32 devices in a mesh: groups: 2 (over x), tok: 16 (over z, y, core).
Axes of the slice: x: 2, y: 2, z: 4, core: 2. Of those that a mesh axis runs over, the one named last changes fastest.
Arguments:
- queries: bfloat16 [4, 3072, 2048], P('groups', 'tok'), parts along dimension 0, may hold values from -6 to 6
- keys: bfloat16 [4, 3072, 2048], P('groups', 'tok'), parts along dimension 0, may hold values from -6 to 6
- values: bfloat16 [4, 3072, 2048], P('groups', 'tok'), parts along dimension 0, may hold values from -6 to 6
- rates: float32 [4, 4, 3072], P('groups', None, 'tok'), parts along dimension 0, may hold values from 4 to 64
- fast_init: bfloat16 [256, 3, 2048], P('tok'), may hold values from -6 to 6
Outputs:
- outputs: bfloat16 [4, 3072, 2048], P('groups', 'tok'), parts along dimension 0
- final_weights: float32 [256, 6, 2048], P('tok', 'groups'), parts along dimension 1
The draws below stay inside these ranges and needn't reach their ends.
There are 2 independent parts, one for each index of `groups`. The reference program is written for one: setup_inputs(seed, part) draws one part's arguments, and reference() takes and returns one part's arrays. A program takes and returns all parts, laid end to end along the dimension named above; an argument that names none is the same for every part. Nothing has to cross between parts.
All inputs are finite; a program needn't handle non-finite values.
Results may differ from the reference program's by a relative error of at most 0.0081.
Values may be sent and summed in bfloat16 or wider, within the bound.
A program may use at most 128 MiB of HBM per device.

```python
import math
import jax
import jax.numpy as jnp
from jax import lax

HEADS = 4
DH = 512
FH = 256
BLOCKS = 2
BLOCK = 3072
HD = 2048


def steps_of(key, extent, split, smallest, largest):
    loudness, own = 1.0, jax.random.fold_in(key, 6)
    for position, parts in split:
        draws = jnp.exp(jax.random.uniform(jax.random.fold_in(own, position), (parts,), jnp.float32, smallest / len(split), largest / len(split)))
        loudness = loudness * jnp.repeat(draws, extent[position] // parts).reshape([-1 if axis == position else 1 for axis in range(len(extent))])
    return loudness


def gaussian(own_key, extent, deviation, reach, cuts=(), dtype=jnp.bfloat16):
    result = deviation * jax.random.normal(own_key, extent, jnp.float32)
    if cuts:
        result = result * steps_of(own_key, extent, cuts, -0.22, 0.18)
    return jnp.clip(result, -reach, reach).astype(dtype)


def setup_inputs(seed: int = 0, part: int = 0) -> dict:
    streams_of = jax.random.split(jax.random.key(seed), 6)
    own_keys = jax.random.split(jax.random.fold_in(streams_of[5], part), 6)
    return {
        "queries": gaussian(own_keys[0], (BLOCKS, BLOCK, HD), 1.0, 6.0, ((1, 16),)),
        "keys": gaussian(own_keys[1], (BLOCKS, BLOCK, HD), 1.0, 6.0, ((1, 16),)),
        "values": gaussian(own_keys[2], (BLOCKS, BLOCK, HD), 1.0, 6.0, ((1, 16),)),
        "rates": jnp.clip(jnp.exp(math.log(64.0) - 2.7725887 * jax.random.uniform(own_keys[3], (BLOCKS, HEADS, BLOCK), jnp.float32) ** steps_of(own_keys[3], (BLOCKS, HEADS, BLOCK), ((2, 16),), -0.2, 0.2)), 4.0, 64.0),
        "fast_init": gaussian(streams_of[4], (FH, 3, HD), 1.0, 6.0, ((0, 16),)),
    }


def project(inputs, weight):
    scale = inputs.shape[2] ** (-0.5)
    return jnp.einsum('thd,fhd->thf', inputs.astype(jnp.float32), weight.astype(jnp.float32)) * scale

def apply_fast(inputs, weight_full, heads):
    tokens = inputs.shape[0]
    hidden = weight_full.shape[0]
    width = inputs.shape[1] // heads
    shaped = inputs.reshape(tokens, heads, width)
    weight = weight_full.reshape(hidden, 3, heads, width)
    first = project(shaped, weight[:, 0])
    second = project(shaped, weight[:, 1])
    gated = (jax.nn.silu(first) * second).astype(jnp.bfloat16)
    mixed = jnp.einsum('thf,fhd->thd', gated.astype(jnp.float32), weight[:, 2].astype(jnp.float32)) * hidden ** (-0.5)
    return mixed.astype(jnp.bfloat16).reshape(tokens, heads * width)

def gradients(keys_rows, scaled_values, weight_full, heads):
    tokens = keys_rows.shape[0]
    hidden = weight_full.shape[0]
    width = keys_rows.shape[1] // heads
    shaped = keys_rows.reshape(tokens, heads, width)
    weight = weight_full.reshape(hidden, 3, heads, width)
    first = project(shaped, weight[:, 0])
    second = project(shaped, weight[:, 1])
    active = jax.nn.silu(first)
    gated = (active * second).astype(jnp.bfloat16)
    back = jnp.einsum('thd,fhd->thf', scaled_values.astype(jnp.float32), weight[:, 2].astype(jnp.float32)) * hidden ** (-0.5)
    sigma = jax.nn.sigmoid(first)
    delta_one = (back * second * sigma * (1.0 + first * (1.0 - sigma))).astype(jnp.bfloat16)
    delta_three = (back * active).astype(jnp.bfloat16)
    kf = shaped.astype(jnp.float32)
    grad_one = jnp.einsum('thf,thd->fhd', delta_one.astype(jnp.float32), kf) * width ** (-0.5)
    grad_three = jnp.einsum('thf,thd->fhd', delta_three.astype(jnp.float32), kf) * width ** (-0.5)
    grad_two = jnp.einsum('thf,thd->fhd', gated.astype(jnp.float32), scaled_values.astype(jnp.float32)) * hidden ** (-0.5)
    return jnp.stack([grad_one, grad_three, grad_two], axis=1).reshape(hidden, 3, heads * width)

def renorm(weight, grad, heads, factor):
    rows = weight.shape[0]
    width = weight.shape[2] // heads
    old = weight.reshape(rows, 3, heads, width)
    moved = old + factor * grad.reshape(rows, 3, heads, width)
    old_norm = jnp.sqrt(lax.optimization_barrier(jnp.sum(old * old, axis=3, keepdims=True)))
    new_norm = jnp.sqrt(lax.optimization_barrier(jnp.sum(moved * moved, axis=3, keepdims=True)) + 1e-06)
    return (moved * old_norm / new_norm).reshape(rows, 3, heads * width)

def reference(queries, keys, values, rates, fast_init):
    factor = BLOCK ** (-0.5)
    state = fast_init.astype(jnp.float32)
    results = []
    for block in range(BLOCKS):
        weight_used = state.astype(jnp.bfloat16)
        results.append(apply_fast(queries[block], weight_used, HEADS))
        shaped_values = values[block].reshape(BLOCK, HEADS, DH).astype(jnp.float32)
        scaled_values = (jnp.transpose(rates[block])[:, :, None] * shaped_values).astype(jnp.bfloat16)
        grad = gradients(keys[block], scaled_values, weight_used, HEADS)
        state = renorm(state, grad, HEADS, factor)
    return (jnp.stack(results, axis=0), state)
```

```python
import functools

import jax
import jax.numpy as jnp
from jax import lax
from jax.experimental import pallas as pl
from jax.experimental.pallas import tpu as pltpu
from jax.sharding import PartitionSpec as P


def project(inputs, weight):
    scale = inputs.shape[2] ** (-0.5)
    return jnp.einsum("thd,fhd->thf", inputs, weight, preferred_element_type=jnp.float32) * scale


def apply_fast(inputs, weight_full, heads):
    tokens = inputs.shape[0]
    hidden = weight_full.shape[0]
    width = inputs.shape[1] // heads
    shaped = inputs.reshape(tokens, heads, width)
    weight = weight_full.reshape(hidden, 3, heads, width)
    first = project(shaped, weight[:, 0])
    second = project(shaped, weight[:, 1])
    gated = (jax.nn.silu(first) * second).astype(jnp.bfloat16)
    mixed = jnp.einsum(
        "thf,fhd->thd", gated, weight[:, 2], preferred_element_type=jnp.float32
    ) * hidden ** (-0.5)
    return mixed.astype(jnp.bfloat16).reshape(tokens, heads * width)


def gradients(keys_rows, scaled_values, weight_full, heads, count):
    tokens = keys_rows.shape[0]
    hidden = weight_full.shape[0]
    width = keys_rows.shape[1] // heads
    shaped = keys_rows.reshape(tokens, heads, width)
    part = weight_full.reshape(count, 3, heads, width)
    first = project(shaped, part[:, 0])
    second = project(shaped, part[:, 1])
    active = jax.nn.silu(first)
    gated = (active * second).astype(jnp.bfloat16)
    back = jnp.einsum(
        "thd,fhd->thf", scaled_values, part[:, 2], preferred_element_type=jnp.float32
    ) * hidden ** (-0.5)
    sigma = jax.nn.sigmoid(first)
    delta_one = (back * second * sigma * (1.0 + first * (1.0 - sigma))).astype(jnp.bfloat16)
    delta_three = (back * active).astype(jnp.bfloat16)
    grad_one = jnp.einsum(
        "thf,thd->fhd", delta_one, shaped, preferred_element_type=jnp.float32
    ) * width ** (-0.5)
    grad_three = jnp.einsum(
        "thf,thd->fhd", delta_three, shaped, preferred_element_type=jnp.float32
    ) * width ** (-0.5)
    grad_two = jnp.einsum(
        "thf,thd->fhd", gated, scaled_values, preferred_element_type=jnp.float32
    ) * hidden ** (-0.5)
    return jnp.stack([grad_one, grad_three, grad_two], axis=1).reshape(count, 3, heads * width)


def renorm(weight, grad, heads, factor):
    rows = weight.shape[0]
    width = weight.shape[2] // heads
    old = weight.reshape(rows, 3, heads, width)
    moved = old + factor * grad.reshape(rows, 3, heads, width)
    old_norm = jnp.sqrt(jnp.sum(old * old, axis=3, keepdims=True))
    new_norm = jnp.sqrt(jnp.sum(moved * moved, axis=3, keepdims=True) + 1e-06)
    return (moved * old_norm / new_norm).reshape(rows, 3, heads * width)


def scale_values(values_rows, rate_rows, heads):
    tokens = values_rows.shape[0]
    width = values_rows.shape[1] // heads
    shaped = values_rows.reshape(tokens, heads, width).astype(jnp.float32)
    return (jnp.transpose(rate_rows)[:, :, None] * shaped).astype(jnp.bfloat16)


def per_device_plain(queries, keys, values, rates, fast_init):
    shards = lax.axis_size("tok")
    heads = rates.shape[1]
    local_rows = fast_init.shape[0]
    all_rows = local_rows * shards
    factor = (keys.shape[1] * shards) ** (-0.5)
    weight_zero = lax.all_gather(fast_init, "tok", axis=0, tiled=True)
    result_zero = apply_fast(queries[0], weight_zero, heads)
    scaled_zero = scale_values(values[0], rates[0], heads)
    summed = lax.psum(gradients(keys[0], scaled_zero, weight_zero, heads, all_rows), "tok")
    state_full = renorm(weight_zero.astype(jnp.float32), summed, heads, factor)
    weight_one = state_full.astype(jnp.bfloat16)
    state_one = lax.dynamic_slice_in_dim(
        state_full, lax.axis_index("tok") * local_rows, local_rows, 0
    )
    result_one = apply_fast(queries[1], weight_one, heads)
    scaled_one = scale_values(values[1], rates[1], heads)
    shares_two = lax.psum_scatter(
        gradients(keys[1], scaled_one, weight_one, heads, lax.axis_size("tok") * local_rows),
        "tok",
        scatter_dimension=0,
        tiled=True,
    )
    state_two = renorm(state_one, shares_two, heads, factor)
    return (jnp.stack([result_zero, result_one], axis=0), state_two)


def dot_nt(a, b):
    return lax.dot_general(a, b, (((1,), (1,)), ((), ())), preferred_element_type=jnp.float32)


def dot_nn(a, b):
    return lax.dot_general(a, b, (((1,), (0,)), ((), ())), preferred_element_type=jnp.float32)


def fused(
    shards, heads, hidden, width, rows, factor,
    q_ref, k_ref, v_ref, rate_ref, init_ref, out_ref, final_ref,
    weights, acc, state, stage, landed, gather_send, gather_recv, sum_send, sum_recv,
):
    me = lax.axis_index("tok")
    bits = shards.bit_length() - 1
    bit = [lax.rem(me // (1 << p), 2) for p in range(bits)]
    partner = [me + (1 << p) * (1 - 2 * bit[p]) for p in range(bits)]
    spans = [hidden >> (p + 1) for p in range(bits)]
    base = [0]
    for p in range(bits):
        base.append(base[p] + bit[p] * spans[p])
    own = pl.multiple_of(base[bits], rows)
    offset = [sum(spans[:p]) for p in range(bits)]

    barrier = pltpu.get_barrier_semaphore()
    for p in range(bits):
        pl.semaphore_signal(
            barrier, inc=1, device_id={"tok": partner[p]}, device_id_type=pl.DeviceIdType.MESH
        )
    pl.semaphore_wait(barrier, bits)

    def gather_copy(block, p, h):
        start = pl.multiple_of(base[p + 1], rows)
        part = weights.at[block, h, pl.ds(start, spans[p]), :]
        return pltpu.make_async_remote_copy(
            src_ref=part,
            dst_ref=part,
            send_sem=gather_send.at[block, p, h],
            recv_sem=gather_recv.at[block, p, h],
            device_id={"tok": partner[p]},
            device_id_type=pl.DeviceIdType.MESH,
        )

    def sum_copy(block, p, h):
        return pltpu.make_async_remote_copy(
            src_ref=stage.at[block, h, pl.ds(offset[p], spans[p]), :],
            dst_ref=landed.at[block, h, pl.ds(offset[p], spans[p]), :],
            send_sem=sum_send.at[block, p, h],
            recv_sem=sum_recv.at[block, p, h],
            device_id={"tok": partner[p]},
            device_id_type=pl.DeviceIdType.MESH,
        )

    def columns(h):
        return slice(h * width, (h + 1) * width)

    def weight(block, h, m):
        return weights[block, h, :, columns(m)]

    wide = width ** (-0.5)
    deep = hidden ** (-0.5)

    def apply_head(block, h):
        x = q_ref[block, :, columns(h)]
        first = dot_nt(x, weight(block, h, 0)) * wide
        second = dot_nt(x, weight(block, h, 1)) * wide
        gated = (first / (1.0 + jnp.exp(-first)) * second).astype(jnp.bfloat16)
        mixed = dot_nn(gated, weight(block, h, 2)) * deep
        out_ref[block, :, columns(h)] = mixed.astype(jnp.bfloat16)

    def gradient_head(block, h):
        k = k_ref[block, :, columns(h)]
        scaled = (rate_ref[block, :, h : h + 1] * v_ref[block, :, columns(h)].astype(jnp.float32)).astype(
            jnp.bfloat16
        )
        first = dot_nt(weight(block, h, 0), k) * wide
        second = dot_nt(weight(block, h, 1), k) * wide
        back = dot_nt(weight(block, h, 2), scaled) * deep
        sigma = 1.0 / (1.0 + jnp.exp(-first))
        active = first * sigma
        gated = (active * second).astype(jnp.bfloat16)
        delta_one = (back * second * sigma * (1.0 + first * (1.0 - sigma))).astype(jnp.bfloat16)
        delta_three = (back * active).astype(jnp.bfloat16)
        acc[h, :, columns(0)] = dot_nn(delta_one, k)
        acc[h, :, columns(1)] = dot_nn(delta_three, k)
        acc[h, :, columns(2)] = dot_nn(gated, scaled)

    def send_sum(block, p, h):
        away = pl.multiple_of(base[p] + (1 - bit[p]) * spans[p], rows)
        total = acc[h, pl.ds(away, spans[p]), :]
        if p > 0:
            before = pl.multiple_of(offset[p - 1] + (1 - bit[p]) * spans[p], rows)
            total = total + landed[block, h, pl.ds(before, spans[p]), :].astype(jnp.float32)
        stage[block, h, offset[p] : offset[p] + spans[p], :] = total.astype(jnp.bfloat16)
        sum_copy(block, p, h).start()
        if p > 0:
            keep = pl.multiple_of(base[p + 1], rows)
            before = pl.multiple_of(offset[p - 1] + bit[p] * spans[p], rows)
            acc[h, pl.ds(keep, spans[p]), :] = acc[h, pl.ds(keep, spans[p]), :] + landed[
                block, h, pl.ds(before, spans[p]), :
            ].astype(jnp.float32)

    def renorm_head(block, h):
        last = bits - 1
        for m, scale in enumerate((wide, wide, deep)):
            grad = acc[h, pl.ds(own, rows), columns(m)] + landed[
                block, h, offset[last] : offset[last] + rows, columns(m)
            ].astype(jnp.float32)
            if block == 0:
                old = init_ref[h, :, columns(m)].astype(jnp.float32)
            else:
                old = state[h, :, columns(m)]
            moved = old + (factor * scale) * grad
            old_norm = jnp.sqrt(jnp.sum(old * old, axis=1, keepdims=True))
            new_norm = jnp.sqrt(jnp.sum(moved * moved, axis=1, keepdims=True) + 1e-06)
            fresh = moved * (old_norm / new_norm)
            if block == 0:
                state[h, :, columns(m)] = fresh
                weights[1, h, pl.ds(own, rows), columns(m)] = fresh.astype(jnp.bfloat16)
            else:
                final_ref[h, :, columns(m)] = fresh

    def gather_step(block, step, h):
        p = bits - 1 - step
        gather_copy(block, p, h).wait_recv()
        if p > 0:
            gather_copy(block, p - 1, h).start()

    for h in range(heads):
        weights[0, h, pl.ds(own, rows), :] = init_ref[h]
        gather_copy(0, bits - 1, h).start()
    for turn in range(heads + bits - 1):
        for step in range(bits - 1, -1, -1):
            h = turn - step
            if 0 <= h < heads:
                gather_step(0, step, h)
                if step == bits - 1:
                    gradient_head(0, h)
                    send_sum(0, 0, h)
    for turn in range(heads + bits - 1):
        for p in range(bits - 1, -1, -1):
            h = turn - p
            if 0 <= h < heads:
                sum_copy(0, p, h).wait_recv()
                if p < bits - 1:
                    send_sum(0, p + 1, h)
                else:
                    renorm_head(0, h)
                    gather_copy(1, bits - 1, h).start()
        if turn < heads:
            apply_head(0, turn)
    for turn in range(heads + bits - 1):
        for step in range(bits - 1, -1, -1):
            h = turn - step
            if 0 <= h < heads:
                gather_step(1, step, h)
                if step == bits - 1:
                    gradient_head(1, h)
                    send_sum(1, 0, h)
    for turn in range(heads + bits - 1):
        for p in range(bits - 1, -1, -1):
            h = turn - p
            if 0 <= h < heads:
                sum_copy(1, p, h).wait_recv()
                if p < bits - 1:
                    send_sum(1, p + 1, h)
                else:
                    renorm_head(1, h)
        if turn < heads:
            apply_head(1, turn)
    for block in range(2):
        for p in range(bits):
            for h in range(heads):
                gather_copy(block, p, h).wait_send()
                sum_copy(block, p, h).wait_send()


def per_device(queries, keys, values, rates, fast_init):
    shards = lax.axis_size("tok")
    heads = rates.shape[1]
    rows = fast_init.shape[0]
    if shards & (shards - 1) or rows % 16:
        return per_device_plain(queries, keys, values, rates, fast_init)
    bits = shards.bit_length() - 1
    blocks, tokens, features = keys.shape
    width = features // heads
    hidden = rows * shards
    factor = (tokens * shards) ** (-0.5)
    start = fast_init.reshape(rows, 3, heads, width).transpose(2, 0, 1, 3).reshape(heads, rows, 3 * width)
    vmem = pl.BlockSpec(memory_space=pltpu.VMEM)
    outputs, final = pl.pallas_call(
        functools.partial(fused, shards, heads, hidden, width, rows, factor),
        out_shape=(
            jax.ShapeDtypeStruct((blocks, tokens, features), jnp.bfloat16),
            jax.ShapeDtypeStruct((heads, rows, 3 * width), jnp.float32),
        ),
        in_specs=[vmem] * 5,
        out_specs=(vmem, vmem),
        scratch_shapes=[
            pltpu.VMEM((2, heads, hidden, 3 * width), jnp.bfloat16),
            pltpu.VMEM((heads, hidden, 3 * width), jnp.float32),
            pltpu.VMEM((heads, rows, 3 * width), jnp.float32),
            pltpu.VMEM((2, heads, hidden - rows, 3 * width), jnp.bfloat16),
            pltpu.VMEM((2, heads, hidden - rows, 3 * width), jnp.bfloat16),
            pltpu.SemaphoreType.DMA((2, bits, heads)),
            pltpu.SemaphoreType.DMA((2, bits, heads)),
            pltpu.SemaphoreType.DMA((2, bits, heads)),
            pltpu.SemaphoreType.DMA((2, bits, heads)),
        ],
        compiler_params=pltpu.CompilerParams(
            collective_id=0, has_side_effects=True, vmem_limit_bytes=52 * 1024 * 1024
        ),
    )(queries, keys, values, jnp.transpose(rates, (0, 2, 1)), start)
    final = final.reshape(heads, rows, 3, width).transpose(1, 2, 0, 3).reshape(rows, 3, features)
    return outputs, final


def solution(mesh):
    in_specs = (
        P("groups", "tok", None),
        P("groups", "tok", None),
        P("groups", "tok", None),
        P("groups", None, "tok"),
        P("tok", None, None),
    )
    out_specs = (P("groups", "tok", None), P("tok", "groups", None))
    return jax.shard_map(
        per_device, mesh=mesh, in_specs=in_specs, out_specs=out_specs, check_vma=False
    )
```

```python
import functools
import heapq

import jax
import jax.numpy as jnp
from jax import lax
from jax.experimental import pallas as pl
from jax.experimental.pallas import tpu as pltpu
from jax.sharding import PartitionSpec as P


def project(inputs, weight):
    scale = inputs.shape[2] ** (-0.5)
    return jnp.einsum("thd,fhd->thf", inputs, weight, preferred_element_type=jnp.float32) * scale


def apply_fast(inputs, weight_full, heads):
    tokens = inputs.shape[0]
    hidden = weight_full.shape[0]
    width = inputs.shape[1] // heads
    shaped = inputs.reshape(tokens, heads, width)
    weight = weight_full.reshape(hidden, 3, heads, width)
    first = project(shaped, weight[:, 0])
    second = project(shaped, weight[:, 1])
    gated = (jax.nn.silu(first) * second).astype(jnp.bfloat16)
    mixed = jnp.einsum(
        "thf,fhd->thd", gated, weight[:, 2], preferred_element_type=jnp.float32
    ) * hidden ** (-0.5)
    return mixed.astype(jnp.bfloat16).reshape(tokens, heads * width)


def gradients(keys_rows, scaled_values, weight_full, heads, count):
    tokens = keys_rows.shape[0]
    hidden = weight_full.shape[0]
    width = keys_rows.shape[1] // heads
    shaped = keys_rows.reshape(tokens, heads, width)
    part = weight_full.reshape(count, 3, heads, width)
    first = project(shaped, part[:, 0])
    second = project(shaped, part[:, 1])
    active = jax.nn.silu(first)
    gated = (active * second).astype(jnp.bfloat16)
    back = jnp.einsum(
        "thd,fhd->thf", scaled_values, part[:, 2], preferred_element_type=jnp.float32
    ) * hidden ** (-0.5)
    sigma = jax.nn.sigmoid(first)
    delta_one = (back * second * sigma * (1.0 + first * (1.0 - sigma))).astype(jnp.bfloat16)
    delta_three = (back * active).astype(jnp.bfloat16)
    grad_one = jnp.einsum(
        "thf,thd->fhd", delta_one, shaped, preferred_element_type=jnp.float32
    ) * width ** (-0.5)
    grad_three = jnp.einsum(
        "thf,thd->fhd", delta_three, shaped, preferred_element_type=jnp.float32
    ) * width ** (-0.5)
    grad_two = jnp.einsum(
        "thf,thd->fhd", gated, scaled_values, preferred_element_type=jnp.float32
    ) * hidden ** (-0.5)
    return jnp.stack([grad_one, grad_three, grad_two], axis=1).reshape(count, 3, heads * width)


def renorm(weight, grad, heads, factor):
    rows = weight.shape[0]
    width = weight.shape[2] // heads
    old = weight.reshape(rows, 3, heads, width)
    moved = old + factor * grad.reshape(rows, 3, heads, width)
    old_norm = jnp.sqrt(jnp.sum(old * old, axis=3, keepdims=True))
    new_norm = jnp.sqrt(jnp.sum(moved * moved, axis=3, keepdims=True) + 1e-06)
    return (moved * old_norm / new_norm).reshape(rows, 3, heads * width)


def scale_values(values_rows, rate_rows, heads):
    tokens = values_rows.shape[0]
    width = values_rows.shape[1] // heads
    shaped = values_rows.reshape(tokens, heads, width).astype(jnp.float32)
    return (jnp.transpose(rate_rows)[:, :, None] * shaped).astype(jnp.bfloat16)


def per_device_plain(queries, keys, values, rates, fast_init):
    shards = lax.axis_size("tok")
    heads = rates.shape[1]
    local_rows = fast_init.shape[0]
    all_rows = local_rows * shards
    factor = (keys.shape[1] * shards) ** (-0.5)
    weight_zero = lax.all_gather(fast_init, "tok", axis=0, tiled=True)
    result_zero = apply_fast(queries[0], weight_zero, heads)
    scaled_zero = scale_values(values[0], rates[0], heads)
    summed = lax.psum(gradients(keys[0], scaled_zero, weight_zero, heads, all_rows), "tok")
    state_full = renorm(weight_zero.astype(jnp.float32), summed, heads, factor)
    weight_one = state_full.astype(jnp.bfloat16)
    state_one = lax.dynamic_slice_in_dim(
        state_full, lax.axis_index("tok") * local_rows, local_rows, 0
    )
    result_one = apply_fast(queries[1], weight_one, heads)
    scaled_one = scale_values(values[1], rates[1], heads)
    shares_two = lax.psum_scatter(
        gradients(keys[1], scaled_one, weight_one, heads, lax.axis_size("tok") * local_rows),
        "tok",
        scatter_dimension=0,
        tiled=True,
    )
    state_two = renorm(state_one, shares_two, heads, factor)
    return (jnp.stack([result_zero, result_one], axis=0), state_two)


PARTS = 3
LATENCY, APPLY, GRAD, ADD = 2.0, 1.2, 2.0, 0.5


def dot_nt(a, b):
    return lax.dot_general(a, b, (((1,), (1,)), ((), ())), preferred_element_type=jnp.float32)


def dot_nn(a, b):
    return lax.dot_general(a, b, (((1,), (0,)), ((), ())), preferred_element_type=jnp.float32)


def fused(
    shards, heads, hidden, width, rows, factor, parts,
    q_ref, k_ref, v_ref, rate_ref, init_ref, out_ref, final_ref,
    weights, acc, state, stage, landed, gather_send, gather_recv, sum_send, sum_recv,
):
    me = lax.axis_index("tok")
    bits = shards.bit_length() - 1
    bit = [lax.rem(me // (1 << p), 2) for p in range(bits)]
    partner = [me + (1 << p) * (1 - 2 * bit[p]) for p in range(bits)]
    spans = [hidden >> (p + 1) for p in range(bits)]
    base = [0]
    for p in range(bits):
        base.append(base[p] + bit[p] * spans[p])
    own = pl.multiple_of(base[bits], rows)
    offset = [sum(spans[:p]) for p in range(bits)]

    barrier = pltpu.get_barrier_semaphore()
    for p in range(bits):
        pl.semaphore_signal(
            barrier, inc=1, device_id={"tok": partner[p]}, device_id_type=pl.DeviceIdType.MESH
        )
    pl.semaphore_wait(barrier, bits)

    def part_of(c):
        h, m = c // parts, c % parts
        size = 3 * width // parts
        return h, slice(m * size, (m + 1) * size)

    def gather_copy(block, p, c):
        h, span = part_of(c)
        start = pl.multiple_of(base[p + 1], rows)
        part = weights.at[block, h, pl.ds(start, spans[p]), span]
        return pltpu.make_async_remote_copy(
            src_ref=part,
            dst_ref=part,
            send_sem=gather_send.at[block, p, c],
            recv_sem=gather_recv.at[block, p, c],
            device_id={"tok": partner[p]},
            device_id_type=pl.DeviceIdType.MESH,
        )

    def sum_copy(block, p, c):
        h, span = part_of(c)
        return pltpu.make_async_remote_copy(
            src_ref=stage.at[block, h, pl.ds(offset[p], spans[p]), span],
            dst_ref=landed.at[block, h, pl.ds(offset[p], spans[p]), span],
            send_sem=sum_send.at[block, p, c],
            recv_sem=sum_recv.at[block, p, c],
            device_id={"tok": partner[p]},
            device_id_type=pl.DeviceIdType.MESH,
        )

    def columns(h):
        return slice(h * width, (h + 1) * width)

    def weight(block, h, m):
        return weights[block, h, :, columns(m)]

    wide = width ** (-0.5)
    deep = hidden ** (-0.5)

    def apply_head(block, h):
        x = q_ref[block, :, columns(h)]
        first = dot_nt(x, weight(block, h, 0)) * wide
        second = dot_nt(x, weight(block, h, 1)) * wide
        gated = (first / (1.0 + jnp.exp(-first)) * second).astype(jnp.bfloat16)
        mixed = dot_nn(gated, weight(block, h, 2)) * deep
        out_ref[block, :, columns(h)] = mixed.astype(jnp.bfloat16)

    def gradient_head(block, h):
        k = k_ref[block, :, columns(h)]
        scaled = (rate_ref[block, :, h : h + 1] * v_ref[block, :, columns(h)].astype(jnp.float32)).astype(
            jnp.bfloat16
        )
        first = dot_nt(weight(block, h, 0), k) * wide
        second = dot_nt(weight(block, h, 1), k) * wide
        back = dot_nt(weight(block, h, 2), scaled) * deep
        sigma = 1.0 / (1.0 + jnp.exp(-first))
        active = first * sigma
        gated = (active * second).astype(jnp.bfloat16)
        delta_one = (back * second * sigma * (1.0 + first * (1.0 - sigma))).astype(jnp.bfloat16)
        delta_three = (back * active).astype(jnp.bfloat16)
        for m, left, right in ((0, delta_one, k), (1, delta_three, k), (2, gated, scaled)):
            acc[h, :, columns(m)] = dot_nn(left, right)

    def send_sum(block, p, c):
        h, span = part_of(c)
        away = pl.multiple_of(base[p] + (1 - bit[p]) * spans[p], rows)
        total = acc[h, pl.ds(away, spans[p]), span]
        if p > 0:
            before = pl.multiple_of(offset[p - 1] + (1 - bit[p]) * spans[p], rows)
            total = total + landed[block, h, pl.ds(before, spans[p]), span].astype(jnp.float32)
        stage[block, h, offset[p] : offset[p] + spans[p], span] = total.astype(jnp.bfloat16)
        sum_copy(block, p, c).start()
        if p > 0:
            keep = pl.multiple_of(base[p + 1], rows)
            before = pl.multiple_of(offset[p - 1] + bit[p] * spans[p], rows)
            acc[h, pl.ds(keep, spans[p]), span] = acc[h, pl.ds(keep, spans[p]), span] + landed[
                block, h, pl.ds(before, spans[p]), span
            ].astype(jnp.float32)

    def renorm_part(block, c):
        last = bits - 1
        h = c // parts
        for m in range(c % parts * 3 // parts, (c % parts + 1) * 3 // parts):
            grad = acc[h, pl.ds(own, rows), columns(m)] + landed[
                block, h, offset[last] : offset[last] + rows, columns(m)
            ].astype(jnp.float32)
            if block == 0:
                old = init_ref[h, :, columns(m)].astype(jnp.float32)
            else:
                old = state[h, :, columns(m)]
            moved = old + (factor * (deep if m == 2 else wide)) * grad
            old_norm = jnp.sqrt(jnp.sum(old * old, axis=1, keepdims=True))
            new_norm = jnp.sqrt(jnp.sum(moved * moved, axis=1, keepdims=True) + 1e-06)
            fresh = moved * (old_norm / new_norm)
            if block == 0:
                state[h, :, columns(m)] = fresh
                weights[1, h, pl.ds(own, rows), columns(m)] = fresh.astype(jnp.bfloat16)
            else:
                final_ref[h, :, columns(m)] = fresh

    piece = rows * 3 * width * 2 / parts
    RATES = (300e3, 50e3, 50e3)
    free = [0.0] * bits
    landing = []
    clock = 0.0
    count = 0
    todo = []
    missing = {}

    def issue(kind, block, p, c):
        nonlocal count
        link = min(p, 2)
        blocks = spans[p] // rows * (2 if p == bits - 1 and p > 1 else 1)
        free[link] = max(free[link], clock) + piece * blocks / RATES[link]
        heapq.heappush(landing, (free[link] + LATENCY, count, kind, block, p, c))
        count += 1

    for h in range(heads):
        weights[0, h, pl.ds(own, rows), :] = init_ref[h]
        for c in range(h * parts, (h + 1) * parts):
            gather_copy(0, bits - 1, c).start()
            issue("gather", 0, bits - 1, c)
    while landing:
        if todo and landing[0][0] > clock + APPLY * 0.5:
            apply_head(*todo.pop(0))
            clock += APPLY
            continue
        at, _, kind, block, p, c = heapq.heappop(landing)
        clock = max(clock, at)
        h = c // parts
        if kind == "gather":
            gather_copy(block, p, c).wait_recv()
            if p > 0:
                gather_copy(block, p - 1, c).start()
                issue("gather", block, p - 1, c)
            else:
                missing[block, h] = missing.get((block, h), parts) - 1
                if missing[block, h] == 0:
                    gradient_head(block, h)
                    clock += GRAD
                    for c in range(h * parts, (h + 1) * parts):
                        send_sum(block, 0, c)
                        clock += ADD / parts
                        issue("sum", block, 0, c)
                    todo.append((block, h))
        else:
            sum_copy(block, p, c).wait_recv()
            if p < bits - 1:
                send_sum(block, p + 1, c)
                clock += ADD / parts / (1 << p)
                issue("sum", block, p + 1, c)
            else:
                renorm_part(block, c)
                clock += 0.3 / parts
                if block == 0:
                    gather_copy(1, bits - 1, c).start()
                    issue("gather", 1, bits - 1, c)
    for item in todo:
        apply_head(*item)
    for block in range(2):
        for p in range(bits):
            for c in range(heads * parts):
                gather_copy(block, p, c).wait_send()
                sum_copy(block, p, c).wait_send()


def per_device(queries, keys, values, rates, fast_init):
    shards = lax.axis_size("tok")
    heads = rates.shape[1]
    rows = fast_init.shape[0]
    if shards & (shards - 1) or rows % 16:
        return per_device_plain(queries, keys, values, rates, fast_init)
    bits = shards.bit_length() - 1
    blocks, tokens, features = keys.shape
    width = features // heads
    hidden = rows * shards
    factor = (tokens * shards) ** (-0.5)
    start = fast_init.reshape(rows, 3, heads, width).transpose(2, 0, 1, 3).reshape(heads, rows, 3 * width)
    vmem = pl.BlockSpec(memory_space=pltpu.VMEM)
    outputs, final = pl.pallas_call(
        functools.partial(fused, shards, heads, hidden, width, rows, factor, PARTS),
        out_shape=(
            jax.ShapeDtypeStruct((blocks, tokens, features), jnp.bfloat16),
            jax.ShapeDtypeStruct((heads, rows, 3 * width), jnp.float32),
        ),
        in_specs=[vmem] * 5,
        out_specs=(vmem, vmem),
        scratch_shapes=[
            pltpu.VMEM((2, heads, hidden, 3 * width), jnp.bfloat16),
            pltpu.VMEM((heads, hidden, 3 * width), jnp.float32),
            pltpu.VMEM((heads, rows, 3 * width), jnp.float32),
            pltpu.VMEM((2, heads, hidden - rows, 3 * width), jnp.bfloat16),
            pltpu.VMEM((2, heads, hidden - rows, 3 * width), jnp.bfloat16),
            pltpu.SemaphoreType.DMA((2, bits, heads * PARTS)),
            pltpu.SemaphoreType.DMA((2, bits, heads * PARTS)),
            pltpu.SemaphoreType.DMA((2, bits, heads * PARTS)),
            pltpu.SemaphoreType.DMA((2, bits, heads * PARTS)),
        ],
        compiler_params=pltpu.CompilerParams(
            collective_id=0, has_side_effects=True, vmem_limit_bytes=52 * 1024 * 1024
        ),
    )(queries, keys, values, jnp.transpose(rates, (0, 2, 1)), start)
    final = final.reshape(heads, rows, 3, width).transpose(1, 2, 0, 3).reshape(rows, 3, features)
    return outputs, final


def solution(mesh):
    in_specs = (
        P("groups", "tok", None),
        P("groups", "tok", None),
        P("groups", "tok", None),
        P("groups", None, "tok"),
        P("tok", None, None),
    )
    out_specs = (P("groups", "tok", None), P("tok", "groups", None))
    return jax.shard_map(
        per_device, mesh=mesh, in_specs=in_specs, out_specs=out_specs, check_vma=False
    )
```

```python
import functools
import heapq

import jax
import jax.numpy as jnp
from jax import lax
from jax.experimental import pallas as pl
from jax.experimental.pallas import tpu as pltpu
from jax.sharding import PartitionSpec as P


def project(inputs, weight):
    scale = inputs.shape[2] ** (-0.5)
    return jnp.einsum("thd,fhd->thf", inputs, weight, preferred_element_type=jnp.float32) * scale


def apply_fast(inputs, weight_full, heads):
    tokens = inputs.shape[0]
    hidden = weight_full.shape[0]
    width = inputs.shape[1] // heads
    shaped = inputs.reshape(tokens, heads, width)
    weight = weight_full.reshape(hidden, 3, heads, width)
    first = project(shaped, weight[:, 0])
    second = project(shaped, weight[:, 1])
    gated = (jax.nn.silu(first) * second).astype(jnp.bfloat16)
    mixed = jnp.einsum(
        "thf,fhd->thd", gated, weight[:, 2], preferred_element_type=jnp.float32
    ) * hidden ** (-0.5)
    return mixed.astype(jnp.bfloat16).reshape(tokens, heads * width)


def gradients(keys_rows, scaled_values, weight_full, heads, count):
    tokens = keys_rows.shape[0]
    hidden = weight_full.shape[0]
    width = keys_rows.shape[1] // heads
    shaped = keys_rows.reshape(tokens, heads, width)
    part = weight_full.reshape(count, 3, heads, width)
    first = project(shaped, part[:, 0])
    second = project(shaped, part[:, 1])
    active = jax.nn.silu(first)
    gated = (active * second).astype(jnp.bfloat16)
    back = jnp.einsum(
        "thd,fhd->thf", scaled_values, part[:, 2], preferred_element_type=jnp.float32
    ) * hidden ** (-0.5)
    sigma = jax.nn.sigmoid(first)
    delta_one = (back * second * sigma * (1.0 + first * (1.0 - sigma))).astype(jnp.bfloat16)
    delta_three = (back * active).astype(jnp.bfloat16)
    grad_one = jnp.einsum(
        "thf,thd->fhd", delta_one, shaped, preferred_element_type=jnp.float32
    ) * width ** (-0.5)
    grad_three = jnp.einsum(
        "thf,thd->fhd", delta_three, shaped, preferred_element_type=jnp.float32
    ) * width ** (-0.5)
    grad_two = jnp.einsum(
        "thf,thd->fhd", gated, scaled_values, preferred_element_type=jnp.float32
    ) * hidden ** (-0.5)
    return jnp.stack([grad_one, grad_three, grad_two], axis=1).reshape(count, 3, heads * width)


def renorm(weight, grad, heads, factor):
    rows = weight.shape[0]
    width = weight.shape[2] // heads
    old = weight.reshape(rows, 3, heads, width)
    moved = old + factor * grad.reshape(rows, 3, heads, width)
    old_norm = jnp.sqrt(jnp.sum(old * old, axis=3, keepdims=True))
    new_norm = jnp.sqrt(jnp.sum(moved * moved, axis=3, keepdims=True) + 1e-06)
    return (moved * old_norm / new_norm).reshape(rows, 3, heads * width)


def scale_values(values_rows, rate_rows, heads):
    tokens = values_rows.shape[0]
    width = values_rows.shape[1] // heads
    shaped = values_rows.reshape(tokens, heads, width).astype(jnp.float32)
    return (jnp.transpose(rate_rows)[:, :, None] * shaped).astype(jnp.bfloat16)


def per_device_plain(queries, keys, values, rates, fast_init):
    shards = lax.axis_size("tok")
    heads = rates.shape[1]
    local_rows = fast_init.shape[0]
    all_rows = local_rows * shards
    factor = (keys.shape[1] * shards) ** (-0.5)
    weight_zero = lax.all_gather(fast_init, "tok", axis=0, tiled=True)
    result_zero = apply_fast(queries[0], weight_zero, heads)
    scaled_zero = scale_values(values[0], rates[0], heads)
    summed = lax.psum(gradients(keys[0], scaled_zero, weight_zero, heads, all_rows), "tok")
    state_full = renorm(weight_zero.astype(jnp.float32), summed, heads, factor)
    weight_one = state_full.astype(jnp.bfloat16)
    state_one = lax.dynamic_slice_in_dim(
        state_full, lax.axis_index("tok") * local_rows, local_rows, 0
    )
    result_one = apply_fast(queries[1], weight_one, heads)
    scaled_one = scale_values(values[1], rates[1], heads)
    shares_two = lax.psum_scatter(
        gradients(keys[1], scaled_one, weight_one, heads, lax.axis_size("tok") * local_rows),
        "tok",
        scatter_dimension=0,
        tiled=True,
    )
    state_two = renorm(state_one, shares_two, heads, factor)
    return (jnp.stack([result_zero, result_one], axis=0), state_two)


PARTS = 3
LATENCY, APPLY, GRAD, ADD = 2.0, 1.2, 2.0, 0.5


def dot_nt(a, b):
    return lax.dot_general(a, b, (((1,), (1,)), ((), ())), preferred_element_type=jnp.float32)


def dot_nn(a, b):
    return lax.dot_general(a, b, (((1,), (0,)), ((), ())), preferred_element_type=jnp.float32)


def fused(
    shards, heads, hidden, width, rows, factor, parts,
    q_hbm, k_hbm, v_hbm, rate_ref, init_ref, out_ref, final_ref,
    q_ref, k_ref, v_ref, load_sem, weights, acc, state, stage, landed, gather_send, gather_recv, sum_send, sum_recv,
    pair_send, pair_recv,
):
    me = lax.axis_index("tok")
    bits = shards.bit_length() - 1
    bit = [lax.rem(me // (1 << p), 2) for p in range(bits)]
    partner = [me + (1 << p) * (1 - 2 * bit[p]) for p in range(bits)]
    spans = [hidden >> (p + 1) for p in range(bits)]
    base = [0]
    for p in range(bits):
        base.append(base[p] + bit[p] * spans[p])
    own = pl.multiple_of(base[bits], rows)
    offset = [sum(spans[:p]) for p in range(bits)]

    paired = lax.axis_size("groups") == 2 and heads >= 2
    group = lax.axis_index("groups")
    pair = (heads - 2, heads - 1) if paired else ()

    barrier = pltpu.get_barrier_semaphore()
    if paired:
        pl.semaphore_signal(
            barrier, inc=1, device_id={"groups": 1 - group}, device_id_type=pl.DeviceIdType.MESH
        )
    for p in range(bits):
        pl.semaphore_signal(
            barrier, inc=1, device_id={"tok": partner[p]}, device_id_type=pl.DeviceIdType.MESH
        )
    pl.semaphore_wait(barrier, bits + int(paired))

    def part_of(c):
        h, m = c // parts, c % parts
        size = 3 * width // parts
        return h, slice(m * size, (m + 1) * size)

    def gather_copy(block, p, c):
        h, span = part_of(c)
        if block == 0 and h in pair:
            h = heads - 2 + group if h == heads - 2 else heads - 1 - group
        start = pl.multiple_of(base[p + 1], rows)
        part = weights.at[block, h, pl.ds(start, spans[p]), span]
        return pltpu.make_async_remote_copy(
            src_ref=part,
            dst_ref=part,
            send_sem=gather_send.at[block, p, c],
            recv_sem=gather_recv.at[block, p, c],
            device_id={"tok": partner[p]},
            device_id_type=pl.DeviceIdType.MESH,
        )

    def pair_copy(c):
        h, span = part_of(c)
        part = weights.at[0, heads - 2 + group, pl.ds(pl.multiple_of(base[1], rows), spans[0]), span]
        return pltpu.make_async_remote_copy(
            src_ref=part,
            dst_ref=part,
            send_sem=pair_send.at[c % parts],
            recv_sem=pair_recv.at[c % parts],
            device_id={"groups": 1 - group},
            device_id_type=pl.DeviceIdType.MESH,
        )

    def sum_copy(block, p, c):
        h, span = part_of(c)
        return pltpu.make_async_remote_copy(
            src_ref=stage.at[block, h, pl.ds(offset[p], spans[p]), span],
            dst_ref=landed.at[block, h, pl.ds(offset[p], spans[p]), span],
            send_sem=sum_send.at[block, p, c],
            recv_sem=sum_recv.at[block, p, c],
            device_id={"tok": partner[p]},
            device_id_type=pl.DeviceIdType.MESH,
        )

    def columns(h):
        return slice(h * width, (h + 1) * width)

    def weight(block, h, m):
        return weights[block, h, :, columns(m)]

    wide = width ** (-0.5)
    deep = hidden ** (-0.5)

    def apply_head(block, h):
        x = q_ref[block, :, columns(h)]
        first = dot_nt(x, weight(block, h, 0)) * wide
        second = dot_nt(x, weight(block, h, 1)) * wide
        gated = (first / (1.0 + jnp.exp(-first)) * second).astype(jnp.bfloat16)
        mixed = dot_nn(gated, weight(block, h, 2)) * deep
        out_ref[block, :, columns(h)] = mixed.astype(jnp.bfloat16)

    def gradient_head(block, h):
        k = k_ref[block, :, columns(h)]
        scaled = (rate_ref[block, :, h : h + 1] * v_ref[block, :, columns(h)].astype(jnp.float32)).astype(
            jnp.bfloat16
        )
        first = dot_nt(weight(block, h, 0), k) * wide
        second = dot_nt(weight(block, h, 1), k) * wide
        back = dot_nt(weight(block, h, 2), scaled) * deep
        sigma = 1.0 / (1.0 + jnp.exp(-first))
        active = first * sigma
        gated = (active * second).astype(jnp.bfloat16)
        delta_one = (back * second * sigma * (1.0 + first * (1.0 - sigma))).astype(jnp.bfloat16)
        delta_three = (back * active).astype(jnp.bfloat16)
        for m, left, right in ((0, delta_one, k), (1, delta_three, k), (2, gated, scaled)):
            acc[h, :, columns(m)] = dot_nn(left, right)

    def send_sum(block, p, c):
        h, span = part_of(c)
        away = pl.multiple_of(base[p] + (1 - bit[p]) * spans[p], rows)
        total = acc[h, pl.ds(away, spans[p]), span]
        if p > 0:
            before = pl.multiple_of(offset[p - 1] + (1 - bit[p]) * spans[p], rows)
            total = total + landed[block, h, pl.ds(before, spans[p]), span].astype(jnp.float32)
        stage[block, h, offset[p] : offset[p] + spans[p], span] = total.astype(jnp.bfloat16)
        sum_copy(block, p, c).start()
        if p > 0:
            keep = pl.multiple_of(base[p + 1], rows)
            before = pl.multiple_of(offset[p - 1] + bit[p] * spans[p], rows)
            acc[h, pl.ds(keep, spans[p]), span] = acc[h, pl.ds(keep, spans[p]), span] + landed[
                block, h, pl.ds(before, spans[p]), span
            ].astype(jnp.float32)

    def renorm_part(block, c):
        last = bits - 1
        h = c // parts
        for m in range(c % parts * 3 // parts, (c % parts + 1) * 3 // parts):
            grad = acc[h, pl.ds(own, rows), columns(m)] + landed[
                block, h, offset[last] : offset[last] + rows, columns(m)
            ].astype(jnp.float32)
            if block == 0:
                old = init_ref[h, :, columns(m)].astype(jnp.float32)
            else:
                old = state[h, :, columns(m)]
            moved = old + (factor * (deep if m == 2 else wide)) * grad
            old_norm = jnp.sqrt(jnp.sum(old * old, axis=1, keepdims=True))
            new_norm = jnp.sqrt(jnp.sum(moved * moved, axis=1, keepdims=True) + 1e-06)
            fresh = moved * (old_norm / new_norm)
            if block == 0:
                state[h, :, columns(m)] = fresh
                weights[1, h, pl.ds(own, rows), columns(m)] = fresh.astype(jnp.bfloat16)
            else:
                final_ref[h, :, columns(m)] = fresh

    piece = rows * 3 * width * 2 / parts
    RATES = (300e3, 50e3, 50e3, 50e3)
    free = [0.0] * 4
    landing = []
    clock = 0.0
    count = 0
    todo = []
    missing = {}

    def issue(kind, block, p, c):
        nonlocal count
        link = 3 if kind == "pair" else min(p, 2)
        blocks = spans[p] // rows * (2 if p == bits - 1 and p > 1 else 1)
        free[link] = max(free[link], clock) + piece * blocks / RATES[link]
        heapq.heappush(landing, (free[link] + LATENCY, count, kind, block, p, c))
        count += 1

    for h in list(pair[:1]) + [h for h in range(heads) if h not in pair]:
        source = heads - 2 + group if h in pair else h
        weights[0, source, pl.ds(own, rows), :] = init_ref[source]
        for c in range(h * parts, (h + 1) * parts):
            gather_copy(0, bits - 1, c).start()
            issue("gather", 0, bits - 1, c)
    loads = [
        pltpu.make_async_copy(source, target, load_sem.at[i])
        for i, (source, target) in enumerate(((k_hbm, k_ref), (v_hbm, v_ref), (q_hbm, q_ref)))
    ]
    for load in loads:
        load.start()
    while landing:
        if todo and landing[0][0] > clock + APPLY * 0.5:
            apply_head(*todo.pop(0))
            clock += APPLY
            continue
        at, _, kind, block, p, c = heapq.heappop(landing)
        clock = max(clock, at)
        h = c // parts
        if kind == "pair":
            pair_copy(c).wait_recv()
            gather_copy(0, 0, c + parts).start()
            issue("gather", 0, 0, c + parts)
        elif kind == "gather":
            gather_copy(block, p, c).wait_recv()
            if p == 1 and block == 0 and h in pair:
                pair_copy(c).start()
                issue("pair", 0, 0, c)
            if p > 0:
                gather_copy(block, p - 1, c).start()
                issue("gather", block, p - 1, c)
            else:
                ready = pair if block == 0 and h in pair else (h,)
                missing[block, ready] = missing.get((block, ready), parts * len(ready)) - 1
                if missing[block, ready] == 0:
                    for load in loads:
                        load.wait()
                    loads = []
                    for h in ready:
                        gradient_head(block, h)
                        clock += GRAD
                        for c in range(h * parts, (h + 1) * parts):
                            send_sum(block, 0, c)
                            clock += ADD / parts
                            issue("sum", block, 0, c)
                        todo.append((block, h))
        else:
            sum_copy(block, p, c).wait_recv()
            if p < bits - 1:
                send_sum(block, p + 1, c)
                clock += ADD / parts / (1 << p)
                issue("sum", block, p + 1, c)
            else:
                renorm_part(block, c)
                clock += 0.3 / parts
                if block == 0:
                    gather_copy(1, bits - 1, c).start()
                    issue("gather", 1, bits - 1, c)
    for item in todo:
        apply_head(*item)
    for block in range(2):
        for p in range(bits):
            for c in range(heads * parts):
                if block or not p or c // parts not in pair[1:]:
                    gather_copy(block, p, c).wait_send()
                sum_copy(block, p, c).wait_send()
    if paired:
        for m in range(parts):
            pair_copy((heads - 2) * parts + m).wait_send()


def per_device(queries, keys, values, rates, fast_init):
    shards = lax.axis_size("tok")
    heads = rates.shape[1]
    rows = fast_init.shape[0]
    if shards & (shards - 1) or rows % 16:
        return per_device_plain(queries, keys, values, rates, fast_init)
    bits = shards.bit_length() - 1
    blocks, tokens, features = keys.shape
    width = features // heads
    hidden = rows * shards
    factor = (tokens * shards) ** (-0.5)
    start = fast_init.reshape(rows, 3, heads, width).transpose(2, 0, 1, 3).reshape(heads, rows, 3 * width)
    vmem = pl.BlockSpec(memory_space=pltpu.VMEM)
    outputs, final = pl.pallas_call(
        functools.partial(fused, shards, heads, hidden, width, rows, factor, PARTS),
        out_shape=(
            jax.ShapeDtypeStruct((blocks, tokens, features), jnp.bfloat16),
            jax.ShapeDtypeStruct((heads, rows, 3 * width), jnp.float32),
        ),
        in_specs=[pl.BlockSpec(memory_space=pl.ANY)] * 3 + [vmem] * 2,
        out_specs=(vmem, vmem),
        scratch_shapes=[
            pltpu.VMEM((blocks, tokens, features), jnp.bfloat16),
            pltpu.VMEM((blocks, tokens, features), jnp.bfloat16),
            pltpu.VMEM((blocks, tokens, features), jnp.bfloat16),
            pltpu.SemaphoreType.DMA((3,)),
            pltpu.VMEM((2, heads, hidden, 3 * width), jnp.bfloat16),
            pltpu.VMEM((heads, hidden, 3 * width), jnp.float32),
            pltpu.VMEM((heads, rows, 3 * width), jnp.float32),
            pltpu.VMEM((2, heads, hidden - rows, 3 * width), jnp.bfloat16),
            pltpu.VMEM((2, heads, hidden - rows, 3 * width), jnp.bfloat16),
            pltpu.SemaphoreType.DMA((2, bits, heads * PARTS)),
            pltpu.SemaphoreType.DMA((2, bits, heads * PARTS)),
            pltpu.SemaphoreType.DMA((2, bits, heads * PARTS)),
            pltpu.SemaphoreType.DMA((2, bits, heads * PARTS)),
            pltpu.SemaphoreType.DMA((PARTS,)),
            pltpu.SemaphoreType.DMA((PARTS,)),
        ],
        compiler_params=pltpu.CompilerParams(
            collective_id=0, has_side_effects=True, vmem_limit_bytes=52 * 1024 * 1024
        ),
    )(queries, keys, values, jnp.transpose(rates, (0, 2, 1)), start)
    final = final.reshape(heads, rows, 3, width).transpose(1, 2, 0, 3).reshape(rows, 3, features)
    return outputs, final


def solution(mesh):
    in_specs = (
        P("groups", "tok", None),
        P("groups", "tok", None),
        P("groups", "tok", None),
        P("groups", None, "tok"),
        P("tok", None, None),
    )
    out_specs = (P("groups", "tok", None), P("tok", "groups", None))
    return jax.shard_map(
        per_device, mesh=mesh, in_specs=in_specs, out_specs=out_specs, check_vma=False
    )
```

```python
import functools
import heapq

import jax
import jax.numpy as jnp
from jax import lax
from jax.experimental import pallas as pl
from jax.experimental.pallas import tpu as pltpu
from jax.sharding import PartitionSpec as P


def project(inputs, weight):
    scale = inputs.shape[2] ** (-0.5)
    return jnp.einsum("thd,fhd->thf", inputs, weight, preferred_element_type=jnp.float32) * scale


def apply_fast(inputs, weight_full, heads):
    tokens = inputs.shape[0]
    hidden = weight_full.shape[0]
    width = inputs.shape[1] // heads
    shaped = inputs.reshape(tokens, heads, width)
    weight = weight_full.reshape(hidden, 3, heads, width)
    first = project(shaped, weight[:, 0])
    second = project(shaped, weight[:, 1])
    gated = (jax.nn.silu(first) * second).astype(jnp.bfloat16)
    mixed = jnp.einsum(
        "thf,fhd->thd", gated, weight[:, 2], preferred_element_type=jnp.float32
    ) * hidden ** (-0.5)
    return mixed.astype(jnp.bfloat16).reshape(tokens, heads * width)


def gradients(keys_rows, scaled_values, weight_full, heads, count):
    tokens = keys_rows.shape[0]
    hidden = weight_full.shape[0]
    width = keys_rows.shape[1] // heads
    shaped = keys_rows.reshape(tokens, heads, width)
    part = weight_full.reshape(count, 3, heads, width)
    first = project(shaped, part[:, 0])
    second = project(shaped, part[:, 1])
    active = jax.nn.silu(first)
    gated = (active * second).astype(jnp.bfloat16)
    back = jnp.einsum(
        "thd,fhd->thf", scaled_values, part[:, 2], preferred_element_type=jnp.float32
    ) * hidden ** (-0.5)
    sigma = jax.nn.sigmoid(first)
    delta_one = (back * second * sigma * (1.0 + first * (1.0 - sigma))).astype(jnp.bfloat16)
    delta_three = (back * active).astype(jnp.bfloat16)
    grad_one = jnp.einsum(
        "thf,thd->fhd", delta_one, shaped, preferred_element_type=jnp.float32
    ) * width ** (-0.5)
    grad_three = jnp.einsum(
        "thf,thd->fhd", delta_three, shaped, preferred_element_type=jnp.float32
    ) * width ** (-0.5)
    grad_two = jnp.einsum(
        "thf,thd->fhd", gated, scaled_values, preferred_element_type=jnp.float32
    ) * hidden ** (-0.5)
    return jnp.stack([grad_one, grad_three, grad_two], axis=1).reshape(count, 3, heads * width)


def renorm(weight, grad, heads, factor):
    rows = weight.shape[0]
    width = weight.shape[2] // heads
    old = weight.reshape(rows, 3, heads, width)
    moved = old + factor * grad.reshape(rows, 3, heads, width)
    old_norm = jnp.sqrt(jnp.sum(old * old, axis=3, keepdims=True))
    new_norm = jnp.sqrt(jnp.sum(moved * moved, axis=3, keepdims=True) + 1e-06)
    return (moved * old_norm / new_norm).reshape(rows, 3, heads * width)


def scale_values(values_rows, rate_rows, heads):
    tokens = values_rows.shape[0]
    width = values_rows.shape[1] // heads
    shaped = values_rows.reshape(tokens, heads, width).astype(jnp.float32)
    return (jnp.transpose(rate_rows)[:, :, None] * shaped).astype(jnp.bfloat16)


def per_device_plain(queries, keys, values, rates, fast_init):
    shards = lax.axis_size("tok")
    heads = rates.shape[1]
    local_rows = fast_init.shape[0]
    all_rows = local_rows * shards
    factor = (keys.shape[1] * shards) ** (-0.5)
    weight_zero = lax.all_gather(fast_init, "tok", axis=0, tiled=True)
    result_zero = apply_fast(queries[0], weight_zero, heads)
    scaled_zero = scale_values(values[0], rates[0], heads)
    summed = lax.psum(gradients(keys[0], scaled_zero, weight_zero, heads, all_rows), "tok")
    state_full = renorm(weight_zero.astype(jnp.float32), summed, heads, factor)
    weight_one = state_full.astype(jnp.bfloat16)
    state_one = lax.dynamic_slice_in_dim(
        state_full, lax.axis_index("tok") * local_rows, local_rows, 0
    )
    result_one = apply_fast(queries[1], weight_one, heads)
    scaled_one = scale_values(values[1], rates[1], heads)
    shares_two = lax.psum_scatter(
        gradients(keys[1], scaled_one, weight_one, heads, lax.axis_size("tok") * local_rows),
        "tok",
        scatter_dimension=0,
        tiled=True,
    )
    state_two = renorm(state_one, shares_two, heads, factor)
    return (jnp.stack([result_zero, result_one], axis=0), state_two)


PARTS = 3
LATENCY, APPLY, GRAD, ADD = 2.0, 1.2, 2.0, 0.5


def dot_nt(a, b):
    return lax.dot_general(a, b, (((1,), (1,)), ((), ())), preferred_element_type=jnp.float32)


def dot_nn(a, b):
    return lax.dot_general(a, b, (((1,), (0,)), ((), ())), preferred_element_type=jnp.float32)


def fused(
    shards, heads, hidden, width, rows, factor, parts,
    q_hbm, k_hbm, v_hbm, rate_ref, init_ref, out_ref, final_ref,
    q_ref, k_ref, v_ref, load_sem, weights, acc, state, stage, landed, gather_send, gather_recv, sum_send, sum_recv,
    pair_send, pair_recv,
):
    me = lax.axis_index("tok")
    bits = shards.bit_length() - 1
    bit = [lax.rem(me // (1 << p), 2) for p in range(bits)]
    partner = [me + (1 << p) * (1 - 2 * bit[p]) for p in range(bits)]
    spans = [hidden >> (p + 1) for p in range(bits)]
    base = [0]
    for p in range(bits):
        base.append(base[p] + bit[p] * spans[p])
    own = pl.multiple_of(base[bits], rows)
    offset = [sum(spans[:p]) for p in range(bits)]

    paired = lax.axis_size("groups") == 2 and heads >= 2
    group = lax.axis_index("groups")
    pair = (heads - 2, heads - 1) if paired else ()

    barrier = pltpu.get_barrier_semaphore()
    if paired:
        pl.semaphore_signal(
            barrier, inc=1, device_id={"groups": 1 - group}, device_id_type=pl.DeviceIdType.MESH
        )
    for p in range(bits):
        pl.semaphore_signal(
            barrier, inc=1, device_id={"tok": partner[p]}, device_id_type=pl.DeviceIdType.MESH
        )
    pl.semaphore_wait(barrier, bits + int(paired))

    def part_of(c):
        h, m = c // parts, c % parts
        size = 3 * width // parts
        return h, slice(m * size, (m + 1) * size)

    def gather_copy(block, p, c):
        h, span = part_of(c)
        if block == 0 and h in pair:
            h = heads - 2 + group if h == heads - 2 else heads - 1 - group
        start = pl.multiple_of(base[p + 1], rows)
        part = weights.at[block, h, pl.ds(start, spans[p]), span]
        return pltpu.make_async_remote_copy(
            src_ref=part,
            dst_ref=part,
            send_sem=gather_send.at[block, p, c],
            recv_sem=gather_recv.at[block, p, c],
            device_id={"tok": partner[p]},
            device_id_type=pl.DeviceIdType.MESH,
        )

    def pair_copy(c):
        h, span = part_of(c)
        part = weights.at[0, heads - 2 + group, pl.ds(pl.multiple_of(base[1], rows), spans[0]), span]
        return pltpu.make_async_remote_copy(
            src_ref=part,
            dst_ref=part,
            send_sem=pair_send.at[c % parts],
            recv_sem=pair_recv.at[c % parts],
            device_id={"groups": 1 - group},
            device_id_type=pl.DeviceIdType.MESH,
        )

    def sum_copy(block, p, c):
        h, span = part_of(c)
        return pltpu.make_async_remote_copy(
            src_ref=stage.at[block, h, pl.ds(offset[p], spans[p]), span],
            dst_ref=landed.at[block, h, pl.ds(offset[p], spans[p]), span],
            send_sem=sum_send.at[block, p, c],
            recv_sem=sum_recv.at[block, p, c],
            device_id={"tok": partner[p]},
            device_id_type=pl.DeviceIdType.MESH,
        )

    def columns(h):
        return slice(h * width, (h + 1) * width)

    def weight(block, h, m):
        return weights[block, h, :, columns(m)]

    wide = width ** (-0.5)
    deep = hidden ** (-0.5)

    def apply_head(block, h):
        x = q_ref[block, :, columns(h)]
        first = dot_nt(x, weight(block, h, 0)) * wide
        second = dot_nt(x, weight(block, h, 1)) * wide
        gated = (first / (1.0 + jnp.exp(-first)) * second).astype(jnp.bfloat16)
        mixed = dot_nn(gated, weight(block, h, 2)) * deep
        out_ref[block, :, columns(h)] = mixed.astype(jnp.bfloat16)

    def gradient_head(block, h):
        k = k_ref[block, :, columns(h)]
        scaled = (rate_ref[block, :, h : h + 1] * v_ref[block, :, columns(h)].astype(jnp.float32)).astype(
            jnp.bfloat16
        )
        first = dot_nt(weight(block, h, 0), k) * wide
        second = dot_nt(weight(block, h, 1), k) * wide
        back = dot_nt(weight(block, h, 2), scaled) * deep
        sigma = 1.0 / (1.0 + jnp.exp(-first))
        active = first * sigma
        gated = (active * second).astype(jnp.bfloat16)
        delta_one = (back * second * sigma * (1.0 + first * (1.0 - sigma))).astype(jnp.bfloat16)
        delta_three = (back * active).astype(jnp.bfloat16)
        for m, left, right in ((0, delta_one, k), (1, delta_three, k), (2, gated, scaled)):
            acc[h, :, columns(m)] = dot_nn(left, right)

    def send_sum(block, p, c):
        h, span = part_of(c)
        away = pl.multiple_of(base[p] + (1 - bit[p]) * spans[p], rows)
        total = acc[h, pl.ds(away, spans[p]), span]
        if p > 0:
            before = pl.multiple_of(offset[p - 1] + (1 - bit[p]) * spans[p], rows)
            total = total + landed[block, h, pl.ds(before, spans[p]), span].astype(jnp.float32)
        stage[block, h, offset[p] : offset[p] + spans[p], span] = total.astype(jnp.bfloat16)
        sum_copy(block, p, c).start()
        if p > 0:
            keep = pl.multiple_of(base[p + 1], rows)
            before = pl.multiple_of(offset[p - 1] + bit[p] * spans[p], rows)
            acc[h, pl.ds(keep, spans[p]), span] = acc[h, pl.ds(keep, spans[p]), span] + landed[
                block, h, pl.ds(before, spans[p]), span
            ].astype(jnp.float32)

    def renorm_part(block, c):
        last = bits - 1
        h = c // parts
        for m in range(c % parts * 3 // parts, (c % parts + 1) * 3 // parts):
            grad = acc[h, pl.ds(own, rows), columns(m)] + landed[
                block, h, offset[last] : offset[last] + rows, columns(m)
            ].astype(jnp.float32)
            if block == 0:
                old = init_ref[h, :, columns(m)].astype(jnp.float32)
            else:
                old = state[h, :, columns(m)]
            moved = old + (factor * (deep if m == 2 else wide)) * grad
            old_norm = jnp.sqrt(jnp.sum(old * old, axis=1, keepdims=True))
            new_norm = jnp.sqrt(jnp.sum(moved * moved, axis=1, keepdims=True) + 1e-06)
            fresh = moved * (old_norm / new_norm)
            if block == 0:
                state[h, :, columns(m)] = fresh
                weights[1, h, pl.ds(own, rows), columns(m)] = fresh.astype(jnp.bfloat16)
            else:
                final_ref[h, :, columns(m)] = fresh

    piece = rows * 3 * width * 2 / parts
    RATES = (300e3, 50e3, 50e3, 50e3)
    free = [0.0] * 4
    landing = []
    clock = 0.0
    count = 0
    todo = []
    missing = {}

    def issue(kind, block, p, c):
        nonlocal count
        link = 3 if kind == "pair" else min(p, 2)
        blocks = spans[p] // rows * (2 if p == bits - 1 and p > 1 else 1)
        free[link] = max(free[link], clock) + piece * blocks / RATES[link]
        heapq.heappush(landing, (free[link] + LATENCY, count, kind, block, p, c))
        count += 1

    for h in [h for h in range(heads) if h not in pair] + list(pair[:1]):
        source = heads - 2 + group if h in pair else h
        weights[0, source, pl.ds(own, rows), :] = init_ref[source]
        for c in range(h * parts, (h + 1) * parts):
            gather_copy(0, bits - 1, c).start()
            issue("gather", 0, bits - 1, c)
    loads = [
        pltpu.make_async_copy(source, target, load_sem.at[i])
        for i, (source, target) in enumerate(((k_hbm, k_ref), (v_hbm, v_ref), (q_hbm, q_ref)))
    ]
    for load in loads:
        load.start()
    while landing:
        if todo and landing[0][0] > clock + APPLY * 0.5:
            apply_head(*todo.pop(0))
            clock += APPLY
            continue
        at, _, kind, block, p, c = heapq.heappop(landing)
        clock = max(clock, at)
        h = c // parts
        if kind == "pair":
            pair_copy(c).wait_recv()
            gather_copy(0, 0, c + parts).start()
            issue("gather", 0, 0, c + parts)
        elif kind == "gather":
            gather_copy(block, p, c).wait_recv()
            if p == 1 and block == 0 and h in pair:
                pair_copy(c).start()
                issue("pair", 0, 0, c)
            if p > 0:
                gather_copy(block, p - 1, c).start()
                issue("gather", block, p - 1, c)
            else:
                ready = pair if block == 0 and h in pair else (h,)
                missing[block, ready] = missing.get((block, ready), parts * len(ready)) - 1
                if missing[block, ready] == 0:
                    for load in loads:
                        load.wait()
                    loads = []
                    for h in ready:
                        gradient_head(block, h)
                        clock += GRAD
                        for c in range(h * parts, (h + 1) * parts):
                            send_sum(block, 0, c)
                            clock += ADD / parts
                            issue("sum", block, 0, c)
                        todo.append((block, h))
        else:
            sum_copy(block, p, c).wait_recv()
            if p < bits - 1:
                send_sum(block, p + 1, c)
                clock += ADD / parts / (1 << p)
                issue("sum", block, p + 1, c)
            else:
                renorm_part(block, c)
                clock += 0.3 / parts
                if block == 0:
                    gather_copy(1, bits - 1, c).start()
                    issue("gather", 1, bits - 1, c)
    for item in todo:
        apply_head(*item)
    for block in range(2):
        for p in range(bits):
            for c in range(heads * parts):
                if block or not p or c // parts not in pair[1:]:
                    gather_copy(block, p, c).wait_send()
                sum_copy(block, p, c).wait_send()
    if paired:
        for m in range(parts):
            pair_copy((heads - 2) * parts + m).wait_send()


def per_device(queries, keys, values, rates, fast_init):
    shards = lax.axis_size("tok")
    heads = rates.shape[1]
    rows = fast_init.shape[0]
    if shards & (shards - 1) or rows % 16:
        return per_device_plain(queries, keys, values, rates, fast_init)
    bits = shards.bit_length() - 1
    blocks, tokens, features = keys.shape
    width = features // heads
    hidden = rows * shards
    factor = (tokens * shards) ** (-0.5)
    start = fast_init.reshape(rows, 3, heads, width).transpose(2, 0, 1, 3).reshape(heads, rows, 3 * width)
    vmem = pl.BlockSpec(memory_space=pltpu.VMEM)
    outputs, final = pl.pallas_call(
        functools.partial(fused, shards, heads, hidden, width, rows, factor, PARTS),
        out_shape=(
            jax.ShapeDtypeStruct((blocks, tokens, features), jnp.bfloat16),
            jax.ShapeDtypeStruct((heads, rows, 3 * width), jnp.float32),
        ),
        in_specs=[pl.BlockSpec(memory_space=pl.ANY)] * 3 + [vmem] * 2,
        out_specs=(vmem, vmem),
        scratch_shapes=[
            pltpu.VMEM((blocks, tokens, features), jnp.bfloat16),
            pltpu.VMEM((blocks, tokens, features), jnp.bfloat16),
            pltpu.VMEM((blocks, tokens, features), jnp.bfloat16),
            pltpu.SemaphoreType.DMA((3,)),
            pltpu.VMEM((2, heads, hidden, 3 * width), jnp.bfloat16),
            pltpu.VMEM((heads, hidden, 3 * width), jnp.float32),
            pltpu.VMEM((heads, rows, 3 * width), jnp.float32),
            pltpu.VMEM((2, heads, hidden - rows, 3 * width), jnp.bfloat16),
            pltpu.VMEM((2, heads, hidden - rows, 3 * width), jnp.bfloat16),
            pltpu.SemaphoreType.DMA((2, bits, heads * PARTS)),
            pltpu.SemaphoreType.DMA((2, bits, heads * PARTS)),
            pltpu.SemaphoreType.DMA((2, bits, heads * PARTS)),
            pltpu.SemaphoreType.DMA((2, bits, heads * PARTS)),
            pltpu.SemaphoreType.DMA((PARTS,)),
            pltpu.SemaphoreType.DMA((PARTS,)),
        ],
        compiler_params=pltpu.CompilerParams(
            collective_id=0, has_side_effects=True, vmem_limit_bytes=52 * 1024 * 1024
        ),
    )(queries, keys, values, jnp.transpose(rates, (0, 2, 1)), start)
    final = final.reshape(heads, rows, 3, width).transpose(1, 2, 0, 3).reshape(rows, 3, features)
    return outputs, final


def solution(mesh):
    in_specs = (
        P("groups", "tok", None),
        P("groups", "tok", None),
        P("groups", "tok", None),
        P("groups", None, "tok"),
        P("tok", None, None),
    )
    out_specs = (P("groups", "tok", None), P("tok", "groups", None))
    return jax.shard_map(
        per_device, mesh=mesh, in_specs=in_specs, out_specs=out_specs, check_vma=False
    )
```
